32 devices in a mesh: dp: 2 (over core), section: 2 (over x), mp: 8 (over z, y).
Axes of the slice: x: 2, y: 2, z: 4, core: 2. Of those that a mesh axis runs over, the one named last changes fastest.
Arguments:
- activations: bfloat16 [2, 2, 128, 32, 384], P('dp', 'section', 'mp'), may hold values from -8 to 8
- out_grads: bfloat16 [2, 2, 128, 32, 384], P('dp', 'section', 'mp'), may hold values from -6 to 6
- layer_weights: bfloat16 [2, 4, 384, 384], P('section'), may hold values from -1.5 to 1.5
Outputs:
- received: bfloat16 [2, 2, 128, 32, 384], P('dp', 'section', 'mp')
- weight_grads: float32 [2, 4, 384, 384], P('section', 'dp', 'mp')
The draws below stay inside these ranges and needn't reach their ends.
All inputs are finite; a program needn't handle non-finite values.
Results may differ from the reference program's by a relative error of at most 0.011.
Values may be sent and summed in bfloat16 or wider, within the bound.
A program may use at most 64 MiB of HBM per device.

```python
import jax
import jax.numpy as jnp
from jax import lax

D = 384
HEADS = 6
HEAD_DIM = 64
SEQS = 128
RES = 32
N_DP = 2
N_SECTION = 2


def draw_activations(key, part):
    shape = (N_DP, N_SECTION, SEQS, RES, D)
    first = jax.random.fold_in(key, 0)
    base = jax.random.normal(first, shape, jnp.float32)
    return jnp.clip(base, -8.0, 8.0).astype(jnp.bfloat16)


def draw_layer_weights(key, part):
    first = jax.random.fold_in(key, 0)
    base = jax.random.normal(first, (N_SECTION, 4, D, HEADS, HEAD_DIM), jnp.float32) * D ** (-0.5)
    return jnp.clip(base.reshape(N_SECTION, 4, D, HEADS * HEAD_DIM), -1.5, 1.5).astype(jnp.bfloat16)


def levels(stream_key, shape, pieces, smallest, top_value):
    factor_of = 1.0
    for position, blocks in pieces:
        draws = jax.random.uniform(jax.random.fold_in(jax.random.fold_in(stream_key, 6), position), (blocks,), jnp.float32, smallest / len(pieces), top_value / len(pieces))
        factor_of = factor_of * jnp.repeat(jnp.exp(draws), shape[position] // blocks).reshape((-1,) + (1,) * (len(shape) - 1 - position))
    return factor_of


def scatter_about(key, dims, spread, bound, shards=(), held_as=jnp.bfloat16):
    result = spread * jax.random.normal(key, dims, jnp.float32)
    if shards:
        result = result * levels(key, dims, shards, -0.22, 0.18)
    return jnp.clip(result, -bound, bound).astype(held_as)


def setup_inputs(seed: int = 0) -> dict:
    key_of = jax.random.split(jax.random.key(seed), 4)
    activations = draw_activations(jax.random.fold_in(key_of[3], 71), 0)
    out_grads = scatter_about(key_of[1], (N_DP, N_SECTION, SEQS, RES, D), 1.0, 6.0, ((0, 2), (1, 2), (2, 8)))
    layer_weights = draw_layer_weights(jax.random.fold_in(key_of[3], 71), 0)
    return {"activations": activations, "out_grads": out_grads, "layer_weights": layer_weights}


EPS = 1e-05

def widen(tensor):
    return lax.optimization_barrier(tensor).astype(jnp.float32)

def normalize(values):
    mean_value = lax.optimization_barrier(jnp.mean(values, axis=-1, keepdims=True))
    centred = values - mean_value
    inverse = lax.rsqrt(lax.optimization_barrier(jnp.mean(centred * centred, axis=-1, keepdims=True)) + EPS)
    return (centred * inverse, inverse)

def norm_backward(grad_in, standard, inverse):
    grad_mean = lax.optimization_barrier(jnp.mean(grad_in, axis=-1, keepdims=True))
    grad_proj = lax.optimization_barrier(jnp.mean(grad_in * standard, axis=-1, keepdims=True))
    return inverse * (grad_in - grad_mean - standard * grad_proj)

def one_column(operands):
    queries, key_rows, values_in, out_delta = operands
    scaling = HEAD_DIM ** (-0.5)
    scores = jnp.einsum('she,the->hst', queries, key_rows) * scaling
    row_max = lax.optimization_barrier(jnp.max(scores, axis=-1, keepdims=True))
    exponent = jnp.exp(scores - row_max)
    probs = exponent / lax.optimization_barrier(jnp.sum(exponent, axis=-1, keepdims=True))
    soft = widen(probs.astype(jnp.bfloat16))
    attn_out = jnp.einsum('hst,the->she', soft, values_in).astype(jnp.bfloat16)
    dprobs = jnp.einsum('she,the->hst', out_delta, values_in)
    row_delta = lax.optimization_barrier(jnp.sum(probs * dprobs, axis=-1, keepdims=True))
    dscores = widen((probs * (dprobs - row_delta)).astype(jnp.bfloat16))
    query_grad = (jnp.einsum('hst,the->she', dscores, key_rows) * scaling).astype(jnp.bfloat16)
    key_grad = (jnp.einsum('hst,she->the', dscores, queries) * scaling).astype(jnp.bfloat16)
    value_grad = jnp.einsum('hst,she->the', soft, out_delta).astype(jnp.bfloat16)
    return (attn_out, query_grad, key_grad, value_grad)

def section_grads(acts, grads_out, weight):
    seq_count, res_count, model_width = acts.shape
    tokens = seq_count * res_count
    head_width = weight.shape[2]
    standard, inverse = normalize(acts.reshape(tokens, model_width).astype(jnp.float32))
    normed = standard.astype(jnp.bfloat16)
    projected = [jnp.dot(normed, weight[slot_index], preferred_element_type=jnp.float32).astype(jnp.bfloat16) for slot_index in range(3)]
    out_flat = grads_out.reshape(tokens, model_width)
    attn_grad = jnp.dot(out_flat, weight[3], preferred_element_type=jnp.float32).astype(jnp.bfloat16)

    def columns(tensor):
        return widen(tensor).reshape(seq_count, res_count, HEADS, HEAD_DIM).transpose(1, 0, 2, 3)
    results = lax.map(one_column, (columns(projected[0]), columns(projected[1]), columns(projected[2]), columns(attn_grad)))

    def flatten(tensor):
        return tensor.transpose(1, 0, 2, 3).reshape(tokens, head_width)
    attn_out, query_grad, key_grad, value_grad = (flatten(tensor) for tensor in results)
    normed_grad = jnp.dot(query_grad, weight[0].T, preferred_element_type=jnp.float32)
    normed_grad = normed_grad + jnp.dot(key_grad, weight[1].T, preferred_element_type=jnp.float32)
    normed_grad = normed_grad + jnp.dot(value_grad, weight[2].T, preferred_element_type=jnp.float32)
    branch = widen(norm_backward(normed_grad, standard, inverse).astype(jnp.bfloat16))
    input_grad = (out_flat.astype(jnp.float32) + branch).astype(jnp.bfloat16).reshape(seq_count, res_count, model_width)
    grads = jnp.stack([jnp.dot(normed.T, query_grad, preferred_element_type=jnp.float32), jnp.dot(normed.T, key_grad, preferred_element_type=jnp.float32), jnp.dot(normed.T, value_grad, preferred_element_type=jnp.float32), jnp.dot(out_flat.T, attn_out, preferred_element_type=jnp.float32)])
    return (input_grad, grads)

def reference(activations, out_grads, layer_weights):
    input_rows = []
    grad_rows = []
    for replica in range(N_DP):
        section_rows = []
        for section_index in range(N_SECTION):
            input_grad, grads = section_grads(activations[replica, section_index], out_grads[replica, section_index], layer_weights[section_index])
            section_rows.append(input_grad)
            if replica == 0:
                grad_rows.append(grads)
            else:
                grad_rows[section_index] = grad_rows[section_index] + grads
        input_rows.append(section_rows)
    received_rows = []
    for replica in range(N_DP):
        shifted = []
        for section_index in range(N_SECTION):
            if section_index + 1 < N_SECTION:
                shifted.append(input_rows[replica][section_index + 1])
            else:
                shifted.append(jnp.zeros_like(input_rows[replica][section_index]))
        received_rows.append(jnp.stack(shifted))
    received = jnp.stack(received_rows)
    weight_grads = jnp.stack(grad_rows)
    return (received, weight_grads)
```

```python
import functools

import jax
import jax.numpy as jnp
from jax import lax
from jax.experimental import pallas as pl
from jax.experimental.pallas import tpu as pltpu
from jax.sharding import PartitionSpec as P

HEAD_DIM = 64


EPS = 1e-05


def passed_along(array, axis, by):
    peers = lax.axis_size(axis)
    pairs = [(i, i + by) for i in range(peers) if 0 <= i + by < peers]
    return lax.ppermute(array, axis, pairs)


def normalize(values):
    mean_value = jnp.mean(values, axis=-1, keepdims=True)
    centred = values - mean_value
    inverse = lax.rsqrt(jnp.mean(centred * centred, axis=-1, keepdims=True) + EPS)
    return (centred * inverse, inverse)


def norm_backward(grad_in, standard, inverse):
    grad_mean = jnp.mean(grad_in, axis=-1, keepdims=True)
    grad_proj = jnp.mean(grad_in * standard, axis=-1, keepdims=True)
    return inverse * (grad_in - grad_mean - standard * grad_proj)


def attend(queries, key_rows, values_in, out_delta):
    seq_count, res_count, head_width = queries.shape
    head_shape = (seq_count, res_count, head_width // HEAD_DIM, HEAD_DIM)
    query_heads = queries.reshape(head_shape)
    key_heads = key_rows.reshape(head_shape)
    value_heads = values_in.reshape(head_shape)
    delta_heads = out_delta.reshape(head_shape)
    scaling = HEAD_DIM ** (-0.5)
    scores = (
        jnp.einsum("srhe,trhe->rhst", query_heads, key_heads, preferred_element_type=jnp.float32)
        * scaling
    )
    row_max = jnp.max(scores, axis=-1, keepdims=True)
    exponent = jnp.exp(scores - row_max)
    probs = exponent / jnp.sum(exponent, axis=-1, keepdims=True)
    soft = probs.astype(jnp.bfloat16)
    attn_out = jnp.einsum(
        "rhst,trhe->srhe", soft, value_heads, preferred_element_type=jnp.float32
    ).astype(jnp.bfloat16)
    dprobs = jnp.einsum(
        "srhe,trhe->rhst", delta_heads, value_heads, preferred_element_type=jnp.float32
    )
    row_delta = jnp.sum(probs * dprobs, axis=-1, keepdims=True)
    dscores = (probs * (dprobs - row_delta)).astype(jnp.bfloat16)
    query_grad = (
        jnp.einsum("rhst,trhe->srhe", dscores, key_heads, preferred_element_type=jnp.float32)
        * scaling
    ).astype(jnp.bfloat16)
    key_grad = (
        jnp.einsum("rhst,srhe->trhe", dscores, query_heads, preferred_element_type=jnp.float32)
        * scaling
    ).astype(jnp.bfloat16)
    value_grad = jnp.einsum(
        "rhst,srhe->trhe", soft, delta_heads, preferred_element_type=jnp.float32
    ).astype(jnp.bfloat16)
    flat_shape = (seq_count, res_count, head_width)
    return (
        attn_out.reshape(flat_shape),
        jnp.stack(
            [
                query_grad.reshape(flat_shape),
                key_grad.reshape(flat_shape),
                value_grad.reshape(flat_shape),
            ]
        ),
    )


def input_gradient(dprojected, weight, standard, inverse, out_flat):
    normed_grad = jnp.einsum(
        "nth,ndh->td", dprojected, weight[:3], preferred_element_type=jnp.float32
    )
    branch = lax.optimization_barrier(
        norm_backward(normed_grad, standard, inverse).astype(jnp.bfloat16)
    )
    return (out_flat.astype(jnp.float32) + branch.astype(jnp.float32)).astype(jnp.bfloat16)


def per_device_plain(activations, out_grads, layer_weights):
    weight = layer_weights[0]
    model_width = activations.shape[4]
    head_width = weight.shape[2]
    col_acts, col_grads = (
        lax.all_to_all(activations, "mp", split_axis=3, concat_axis=2, tiled=True),
        lax.all_to_all(out_grads, "mp", split_axis=3, concat_axis=2, tiled=True),
    )
    seq_count, res_count = (col_acts.shape[2], col_acts.shape[3])
    tokens = seq_count * res_count
    standard, inverse = normalize(col_acts.reshape(tokens, model_width).astype(jnp.float32))
    normed = standard.astype(jnp.bfloat16)
    out_flat = col_grads.reshape(tokens, model_width)
    projected = jnp.einsum(
        "td,ndh->nth", normed, weight[:3], preferred_element_type=jnp.float32
    ).astype(jnp.bfloat16)
    attn_grad = jnp.dot(out_flat, weight[3], preferred_element_type=jnp.float32).astype(
        jnp.bfloat16
    )
    grid_shape = (seq_count, res_count, head_width)
    attn_out, stacked_grads = attend(
        projected[0].reshape(grid_shape),
        projected[1].reshape(grid_shape),
        projected[2].reshape(grid_shape),
        attn_grad.reshape(grid_shape),
    )
    dprojected = stacked_grads.reshape(3, tokens, head_width)
    attn_flat = attn_out.reshape(tokens, head_width)
    input_grad = input_gradient(dprojected, weight, standard, inverse, out_flat)
    row_grads = lax.all_to_all(
        input_grad.reshape(col_acts.shape), "mp", split_axis=2, concat_axis=3, tiled=True
    )
    received = passed_along(row_grads, "section", -1)
    projection_terms = jnp.einsum(
        "td,nth->ndh", normed, dprojected, preferred_element_type=jnp.float32
    )
    output_term = jnp.einsum("td,th->dh", out_flat, attn_flat, preferred_element_type=jnp.float32)
    grad_term = jnp.concatenate([projection_terms, output_term[None]], axis=0)[None]
    model_part = lax.psum_scatter(grad_term, "mp", scatter_dimension=2, tiled=True)
    replica_part = lax.psum_scatter(model_part, "dp", scatter_dimension=1, tiled=True)
    return (received, replica_part)


MESH = pl.DeviceIdType.MESH
LANES = 128
ROWS = 16
F32 = jnp.float32
BF16 = jnp.bfloat16


def dot_t(left, right):
    return lax.dot_general(left, right, (((1,), (1,)), ((), ())), preferred_element_type=F32)


def t_dot(left, right):
    return lax.dot_general(left, right, (((0,), (0,)), ((), ())), preferred_element_type=F32)


def attend_pair(query, key, value, delta):
    count = LANES // HEAD_DIM
    seqs = query.shape[0]
    scaling = HEAD_DIM ** (-0.5)
    lane = lax.broadcasted_iota(jnp.int32, (seqs, LANES), 1)
    masks = [(lane >= h * HEAD_DIM) & (lane < (h + 1) * HEAD_DIM) for h in range(count)]
    zero = jnp.zeros_like(key)
    keys = jnp.concatenate([jnp.where(m, key, zero) for m in masks], axis=0)
    values = jnp.concatenate([jnp.where(m, value, zero) for m in masks], axis=0)
    scores = dot_t(query, keys)
    dprobs = dot_t(delta, values)
    softs, dscores = [], []
    for h in range(count):
        cut = slice(h * seqs, (h + 1) * seqs)
        score = scores[:, cut] * scaling
        exponent = jnp.exp(score - jnp.max(score, axis=-1, keepdims=True))
        probs = exponent * (1.0 / jnp.sum(exponent, axis=-1, keepdims=True))
        dprob = dprobs[:, cut]
        row_delta = jnp.sum(probs * dprob, axis=-1, keepdims=True)
        softs.append(probs.astype(BF16))
        dscores.append((probs * (dprob - row_delta)).astype(BF16))
    soft = jnp.concatenate(softs, axis=1)
    dscore = jnp.concatenate(dscores, axis=1)
    out = jnp.dot(soft, values, preferred_element_type=F32)
    query_grad = jnp.dot(dscore, keys, preferred_element_type=F32) * scaling
    key_grad = t_dot(dscores[0], query)
    value_grad = t_dot(softs[0], delta)
    for h in range(1, count):
        key_grad = jnp.where(masks[h], t_dot(dscores[h], query), key_grad)
        value_grad = jnp.where(masks[h], t_dot(softs[h], delta), value_grad)
    key_grad = key_grad * scaling
    return query_grad.astype(BF16), key_grad.astype(BF16), value_grad.astype(BF16), out.astype(BF16)


def kernel(
    n_mp, n_section, n_dp, acts_ref, grads_ref, w_ref, got_ref, wout_ref,
    cols, lefts, rights, back, part, other, mine, share, landed,
    col_send, col_recv, back_send, back_recv, dp_send, dp_recv, mp_send, mp_recv,
):
    me = lax.axis_index("mp")
    section = lax.axis_index("section")
    replica = lax.axis_index("dp")
    columns, _, seqs, width = acts_ref.shape
    tokens = n_mp * seqs
    slots = wout_ref.shape[0]
    rows = wout_ref.shape[1]
    sends_back = section > 0
    gets_back = section < n_section - 1

    def peer(k):
        return lax.rem(me + k, n_mp)

    def source(k):
        return lax.rem(me + n_mp - k, n_mp)

    def col_copy(which, c, k):
        ref = acts_ref if which == 0 else grads_ref
        return pltpu.make_async_remote_copy(
            src_ref=ref.at[c, peer(k)], dst_ref=cols.at[which, c, me],
            send_sem=col_send.at[which, c, k], recv_sem=col_recv.at[which, c, me],
            device_id={"mp": peer(k)}, device_id_type=MESH)

    def col_wait(which, c, k):
        return pltpu.make_async_remote_copy(
            src_ref=acts_ref.at[c, me], dst_ref=cols.at[which, c, source(k)],
            send_sem=col_send.at[which, c, k], recv_sem=col_recv.at[which, c, source(k)],
            device_id={"mp": peer(k)}, device_id_type=MESH)

    def back_copy(c, p):
        return pltpu.make_async_remote_copy(
            src_ref=back.at[c, p], dst_ref=got_ref.at[c, me],
            send_sem=back_send.at[c, p], recv_sem=back_recv.at[c, me],
            device_id={"section": jnp.maximum(section - 1, 0), "mp": p}, device_id_type=MESH)

    def back_wait(c, p):
        return pltpu.make_async_remote_copy(
            src_ref=back.at[c, p], dst_ref=got_ref.at[c, p],
            send_sem=back_send.at[c, p], recv_sem=back_recv.at[c, p],
            device_id={"section": jnp.maximum(section - 1, 0), "mp": p}, device_id_type=MESH)

    def dp_copy(j):
        return pltpu.make_async_remote_copy(
            src_ref=part.at[j], dst_ref=other.at[j],
            send_sem=dp_send.at[j], recv_sem=dp_recv.at[j],
            device_id={"dp": 1 - replica}, device_id_type=MESH)

    def mp_copy(j, k):
        return pltpu.make_async_remote_copy(
            src_ref=share.at[j, peer(k)], dst_ref=landed.at[j, me],
            send_sem=mp_send.at[j, k], recv_sem=mp_recv.at[j, me],
            device_id={"mp": peer(k)}, device_id_type=MESH)

    def mp_wait(j, k):
        return pltpu.make_async_remote_copy(
            src_ref=share.at[j, me], dst_ref=landed.at[j, source(k)],
            send_sem=mp_send.at[j, k], recv_sem=mp_recv.at[j, source(k)],
            device_id={"mp": peer(k)}, device_id_type=MESH)

    barrier = pltpu.get_barrier_semaphore()

    @pl.loop(1, n_mp)
    def _(k):
        pl.semaphore_signal(barrier, inc=1, device_id={"mp": peer(k)}, device_id_type=MESH)

    pl.semaphore_signal(barrier, inc=1, device_id={"dp": 1 - replica}, device_id_type=MESH)

    @pl.when(sends_back)
    def _():
        @pl.loop(0, n_mp)
        def _(p):
            pl.semaphore_signal(
                barrier, inc=1, device_id={"section": section - 1, "mp": p}, device_id_type=MESH)

    @pl.when(gets_back)
    def _():
        @pl.loop(0, n_mp)
        def _(p):
            pl.semaphore_signal(
                barrier, inc=1, device_id={"section": section + 1, "mp": p}, device_id_type=MESH)

    neighbours = (section > 0).astype(jnp.int32) + (section < n_section - 1).astype(jnp.int32)
    pl.semaphore_wait(barrier, n_mp + n_mp * neighbours)

    @pl.loop(0, columns)
    def _(c):
        @pl.loop(1, n_mp)
        def _(k):
            col_copy(0, c, k).start()
            col_copy(1, c, k).start()

    @pl.loop(0, columns)
    def _(c):
        cols[0, c, me] = acts_ref[c, me]
        cols[1, c, me] = grads_ref[c, me]

    @pl.when(jnp.logical_not(gets_back))
    def _():
        got_ref[...] = jnp.zeros_like(got_ref)

    @pl.loop(0, columns)
    def _(c):
        @pl.loop(1, n_mp)
        def _(k):
            col_wait(0, c, k).wait_recv()
            col_wait(1, c, k).wait_recv()

        standard, inverse = normalize(cols[0, c].reshape(tokens, width).astype(F32))
        normed = standard.astype(BF16)
        out_flat = cols[1, c].reshape(tokens, width)
        lefts[0, c] = normed
        lefts[1, c] = out_flat
        query, key, value = (
            jnp.dot(normed, w_ref[n], preferred_element_type=F32).astype(BF16) for n in range(3))
        delta = jnp.dot(out_flat, w_ref[3], preferred_element_type=F32).astype(BF16)
        for t in range(query.shape[1] // LANES):
            cut = slice(t * LANES, (t + 1) * LANES)
            results = attend_pair(query[:, cut], key[:, cut], value[:, cut], delta[:, cut])
            for n in range(4):
                rights[n, c, :, cut] = results[n]

        @pl.when(sends_back)
        def _():
            normed_grad = dot_t(rights[0, c], w_ref[0])
            normed_grad += dot_t(rights[1, c], w_ref[1])
            normed_grad += dot_t(rights[2, c], w_ref[2])
            branch = norm_backward(normed_grad, standard, inverse).astype(BF16)
            total = (out_flat.astype(F32) + branch.astype(F32)).astype(BF16)
            back[c] = total.reshape(n_mp, seqs, width)

            @pl.loop(0, n_mp)
            def _(p):
                back_copy(c, p).start()

    def weight_grad(slot):
        left = lefts[slot // 3].reshape(columns * tokens, width)
        right = rights[slot].reshape(columns * tokens, rights.shape[-1])
        return t_dot(left, right)

    for j in range(slots):
        grad = weight_grad((1 - replica) * slots + j)
        part[j] = grad.reshape(part.shape[1:]).astype(part.dtype)
        dp_copy(j).start()
    for j in range(slots):
        mine[j] = weight_grad(replica * slots + j).reshape(mine.shape[1:])
    for j in range(slots):
        dp_copy(j).wait()
        summed = mine[j] + other[j].astype(F32)
        mine[j] = summed
        share[j] = summed.astype(share.dtype)

        @pl.loop(1, n_mp)
        def _(k):
            mp_copy(j, k).start()

    for j in range(slots):
        wout_ref[j] = mine[j, me]

        @pl.loop(1, n_mp)
        def _(k):
            mp_wait(j, k).wait_recv()
            wout_ref[j] += landed[j, source(k)].astype(F32)

    @pl.when(gets_back)
    def _():
        @pl.loop(0, columns)
        def _(c):
            @pl.loop(0, n_mp)
            def _(p):
                back_wait(c, p).wait_recv()

    @pl.when(sends_back)
    def _():
        @pl.loop(0, columns)
        def _(c):
            @pl.loop(0, n_mp)
            def _(p):
                back_copy(c, p).wait_send()

    @pl.loop(1, n_mp)
    def _(k):
        @pl.loop(0, columns)
        def _(c):
            col_copy(0, c, k).wait_send()
            col_copy(1, c, k).wait_send()

        for j in range(slots):
            mp_copy(j, k).wait_send()


def per_device_kernel(activations, out_grads, layer_weights):
    n_mp, n_section, n_dp = (lax.axis_size(name) for name in ("mp", "section", "dp"))
    _, _, seqs, residues, width = activations.shape
    columns = residues // n_mp
    head_width = layer_weights.shape[3]
    tokens = n_mp * seqs
    kinds = layer_weights.shape[1]
    slots, rows = kinds // n_dp, width // n_mp

    def by_column(array):
        cut = array.reshape(seqs, n_mp, columns, width)
        return cut.transpose(2, 1, 0, 3)

    vmem = pl.BlockSpec(memory_space=pltpu.VMEM)
    dma = pltpu.SemaphoreType.DMA
    pieces = (slots, n_mp, rows, head_width)
    got, weight_grads = pl.pallas_call(
        functools.partial(kernel, n_mp, n_section, n_dp),
        out_shape=(
            jax.ShapeDtypeStruct((columns, n_mp, seqs, width), BF16),
            jax.ShapeDtypeStruct((slots, rows, head_width), F32),
        ),
        in_specs=[vmem] * 3,
        out_specs=(vmem, vmem),
        scratch_shapes=[
            pltpu.VMEM((2, columns, n_mp, seqs, width), BF16),
            pltpu.VMEM((2, columns, tokens, width), BF16),
            pltpu.VMEM((kinds, columns, tokens, head_width), BF16),
            pltpu.VMEM((columns, n_mp, seqs, width), BF16),
            pltpu.VMEM(pieces, BF16),
            pltpu.VMEM(pieces, BF16),
            pltpu.VMEM(pieces, F32),
            pltpu.VMEM(pieces, BF16),
            pltpu.VMEM(pieces, BF16),
            dma((2, columns, n_mp)),
            dma((2, columns, n_mp)),
            dma((columns, n_mp)),
            dma((columns, n_mp)),
            dma((slots,)),
            dma((slots,)),
            dma((slots, n_mp)),
            dma((slots, n_mp)),
        ],
        compiler_params=pltpu.CompilerParams(
            collective_id=0, has_side_effects=True, vmem_limit_bytes=48 * 1024 * 1024),
    )(by_column(activations), by_column(out_grads), layer_weights[0])
    received = got.transpose(2, 1, 0, 3).reshape(activations.shape)
    return received, weight_grads[None]


def per_device(activations, out_grads, layer_weights):
    n_mp, n_dp = lax.axis_size("mp"), lax.axis_size("dp")
    _, kinds, width, head_width = layer_weights.shape
    fits = (
        n_dp == 2
        and kinds % n_dp == 0
        and n_mp > 1
        and activations.shape[2] % ROWS == 0
        and (width // n_mp) % ROWS == 0
        and head_width % LANES == 0
    )
    body = per_device_kernel if fits else per_device_plain
    return body(activations, out_grads, layer_weights)


def solution(mesh):
    in_specs = (
        P("dp", "section", "mp", None, None),
        P("dp", "section", "mp", None, None),
        P("section", None, None, None),
    )
    out_specs = (P("dp", "section", "mp", None, None), P("section", "dp", "mp", None))
    return jax.shard_map(
        per_device, mesh=mesh, in_specs=in_specs, out_specs=out_specs, check_vma=False
    )
```

```python
import functools

import jax
import jax.numpy as jnp
from jax import lax
from jax.experimental import pallas as pl
from jax.experimental.pallas import tpu as pltpu
from jax.sharding import PartitionSpec as P

HEAD_DIM = 64


EPS = 1e-05


def passed_along(array, axis, by):
    peers = lax.axis_size(axis)
    pairs = [(i, i + by) for i in range(peers) if 0 <= i + by < peers]
    return lax.ppermute(array, axis, pairs)


def normalize(values):
    mean_value = jnp.mean(values, axis=-1, keepdims=True)
    centred = values - mean_value
    inverse = lax.rsqrt(jnp.mean(centred * centred, axis=-1, keepdims=True) + EPS)
    return (centred * inverse, inverse)


def norm_backward(grad_in, standard, inverse):
    grad_mean = jnp.mean(grad_in, axis=-1, keepdims=True)
    grad_proj = jnp.mean(grad_in * standard, axis=-1, keepdims=True)
    return inverse * (grad_in - grad_mean - standard * grad_proj)


def attend(queries, key_rows, values_in, out_delta):
    seq_count, res_count, head_width = queries.shape
    head_shape = (seq_count, res_count, head_width // HEAD_DIM, HEAD_DIM)
    query_heads = queries.reshape(head_shape)
    key_heads = key_rows.reshape(head_shape)
    value_heads = values_in.reshape(head_shape)
    delta_heads = out_delta.reshape(head_shape)
    scaling = HEAD_DIM ** (-0.5)
    scores = (
        jnp.einsum("srhe,trhe->rhst", query_heads, key_heads, preferred_element_type=jnp.float32)
        * scaling
    )
    row_max = jnp.max(scores, axis=-1, keepdims=True)
    exponent = jnp.exp(scores - row_max)
    probs = exponent / jnp.sum(exponent, axis=-1, keepdims=True)
    soft = probs.astype(jnp.bfloat16)
    attn_out = jnp.einsum(
        "rhst,trhe->srhe", soft, value_heads, preferred_element_type=jnp.float32
    ).astype(jnp.bfloat16)
    dprobs = jnp.einsum(
        "srhe,trhe->rhst", delta_heads, value_heads, preferred_element_type=jnp.float32
    )
    row_delta = jnp.sum(probs * dprobs, axis=-1, keepdims=True)
    dscores = (probs * (dprobs - row_delta)).astype(jnp.bfloat16)
    query_grad = (
        jnp.einsum("rhst,trhe->srhe", dscores, key_heads, preferred_element_type=jnp.float32)
        * scaling
    ).astype(jnp.bfloat16)
    key_grad = (
        jnp.einsum("rhst,srhe->trhe", dscores, query_heads, preferred_element_type=jnp.float32)
        * scaling
    ).astype(jnp.bfloat16)
    value_grad = jnp.einsum(
        "rhst,srhe->trhe", soft, delta_heads, preferred_element_type=jnp.float32
    ).astype(jnp.bfloat16)
    flat_shape = (seq_count, res_count, head_width)
    return (
        attn_out.reshape(flat_shape),
        jnp.stack(
            [
                query_grad.reshape(flat_shape),
                key_grad.reshape(flat_shape),
                value_grad.reshape(flat_shape),
            ]
        ),
    )


def input_gradient(dprojected, weight, standard, inverse, out_flat):
    normed_grad = jnp.einsum(
        "nth,ndh->td", dprojected, weight[:3], preferred_element_type=jnp.float32
    )
    branch = lax.optimization_barrier(
        norm_backward(normed_grad, standard, inverse).astype(jnp.bfloat16)
    )
    return (out_flat.astype(jnp.float32) + branch.astype(jnp.float32)).astype(jnp.bfloat16)


def per_device_plain(activations, out_grads, layer_weights):
    weight = layer_weights[0]
    model_width = activations.shape[4]
    head_width = weight.shape[2]
    col_acts, col_grads = (
        lax.all_to_all(activations, "mp", split_axis=3, concat_axis=2, tiled=True),
        lax.all_to_all(out_grads, "mp", split_axis=3, concat_axis=2, tiled=True),
    )
    seq_count, res_count = (col_acts.shape[2], col_acts.shape[3])
    tokens = seq_count * res_count
    standard, inverse = normalize(col_acts.reshape(tokens, model_width).astype(jnp.float32))
    normed = standard.astype(jnp.bfloat16)
    out_flat = col_grads.reshape(tokens, model_width)
    projected = jnp.einsum(
        "td,ndh->nth", normed, weight[:3], preferred_element_type=jnp.float32
    ).astype(jnp.bfloat16)
    attn_grad = jnp.dot(out_flat, weight[3], preferred_element_type=jnp.float32).astype(
        jnp.bfloat16
    )
    grid_shape = (seq_count, res_count, head_width)
    attn_out, stacked_grads = attend(
        projected[0].reshape(grid_shape),
        projected[1].reshape(grid_shape),
        projected[2].reshape(grid_shape),
        attn_grad.reshape(grid_shape),
    )
    dprojected = stacked_grads.reshape(3, tokens, head_width)
    attn_flat = attn_out.reshape(tokens, head_width)
    input_grad = input_gradient(dprojected, weight, standard, inverse, out_flat)
    row_grads = lax.all_to_all(
        input_grad.reshape(col_acts.shape), "mp", split_axis=2, concat_axis=3, tiled=True
    )
    received = passed_along(row_grads, "section", -1)
    projection_terms = jnp.einsum(
        "td,nth->ndh", normed, dprojected, preferred_element_type=jnp.float32
    )
    output_term = jnp.einsum("td,th->dh", out_flat, attn_flat, preferred_element_type=jnp.float32)
    grad_term = jnp.concatenate([projection_terms, output_term[None]], axis=0)[None]
    model_part = lax.psum_scatter(grad_term, "mp", scatter_dimension=2, tiled=True)
    replica_part = lax.psum_scatter(model_part, "dp", scatter_dimension=1, tiled=True)
    return (received, replica_part)


MESH = pl.DeviceIdType.MESH
LANES = 128
ROWS = 16
F32 = jnp.float32
BF16 = jnp.bfloat16


def dot_t(left, right):
    return lax.dot_general(left, right, (((1,), (1,)), ((), ())), preferred_element_type=F32)


def t_dot(left, right):
    return lax.dot_general(left, right, (((0,), (0,)), ((), ())), preferred_element_type=F32)


def attend_pair(query, key, value, delta):
    count = LANES // HEAD_DIM
    seqs = query.shape[0]
    scaling = HEAD_DIM ** (-0.5)
    lane = lax.broadcasted_iota(jnp.int32, (seqs, LANES), 1)
    masks = [(lane >= h * HEAD_DIM) & (lane < (h + 1) * HEAD_DIM) for h in range(count)]
    zero = jnp.zeros_like(key)
    keys = jnp.concatenate([jnp.where(m, key, zero) for m in masks], axis=0)
    values = jnp.concatenate([jnp.where(m, value, zero) for m in masks], axis=0)
    scores = dot_t(query, keys)
    dprobs = dot_t(delta, values)
    softs, dscores = [], []
    for h in range(count):
        cut = slice(h * seqs, (h + 1) * seqs)
        score = scores[:, cut] * scaling
        exponent = jnp.exp(score - jnp.max(score, axis=-1, keepdims=True))
        probs = exponent * (1.0 / jnp.sum(exponent, axis=-1, keepdims=True))
        dprob = dprobs[:, cut]
        row_delta = jnp.sum(probs * dprob, axis=-1, keepdims=True)
        softs.append(probs.astype(BF16))
        dscores.append((probs * (dprob - row_delta)).astype(BF16))
    soft = jnp.concatenate(softs, axis=1)
    dscore = jnp.concatenate(dscores, axis=1)
    out = jnp.dot(soft, values, preferred_element_type=F32)
    query_grad = jnp.dot(dscore, keys, preferred_element_type=F32) * scaling
    key_grad = t_dot(dscores[0], query)
    value_grad = t_dot(softs[0], delta)
    for h in range(1, count):
        key_grad = jnp.where(masks[h], t_dot(dscores[h], query), key_grad)
        value_grad = jnp.where(masks[h], t_dot(softs[h], delta), value_grad)
    key_grad = key_grad * scaling
    return query_grad.astype(BF16), key_grad.astype(BF16), value_grad.astype(BF16), out.astype(BF16)


def kernel(
    n_mp, n_section, n_dp, acts_ref, grads_ref, w_ref, got_ref, wout_ref,
    both, cols, lefts, rights, back, part, other, mine, share, landed, total, ysend, yland,
    col_send, col_recv, back_send, back_recv, dp_send, dp_recv, mp_send, mp_recv, y_send, y_recv,
):
    me = lax.axis_index("mp")
    section = lax.axis_index("section")
    replica = lax.axis_index("dp")
    columns, _, seqs, width = acts_ref.shape
    tokens = n_mp * seqs
    slots = wout_ref.shape[0]
    rows = wout_ref.shape[1]
    sends_back = section > 0
    gets_back = section < n_section - 1
    halves = n_mp // 2
    half, parity = me // 2, lax.rem(me, 2)

    def peer(k):
        return lax.rem(me + k, n_mp)

    def source(k):
        return lax.rem(me + n_mp - k, n_mp)

    others = pl.ds(0, n_mp - 1)

    def col_copy(c, k):
        return pltpu.make_async_remote_copy(
            src_ref=both.at[c, peer(k)], dst_ref=cols.at[c, me],
            send_sem=col_send, recv_sem=col_recv.at[c],
            device_id={"mp": peer(k)}, device_id_type=MESH)

    def col_all(c):
        return pltpu.make_async_remote_copy(
            src_ref=both.at[:, others], dst_ref=cols.at[c, others],
            send_sem=col_send, recv_sem=col_recv.at[c],
            device_id={"mp": peer(1)}, device_id_type=MESH)

    def back_copy(c, p):
        return pltpu.make_async_remote_copy(
            src_ref=back.at[c, p], dst_ref=got_ref.at[c, me],
            send_sem=back_send, recv_sem=back_recv,
            device_id={"section": jnp.maximum(section - 1, 0), "mp": p}, device_id_type=MESH)

    def back_all():
        return pltpu.make_async_remote_copy(
            src_ref=back, dst_ref=got_ref, send_sem=back_send, recv_sem=back_recv,
            device_id={"section": jnp.maximum(section - 1, 0)}, device_id_type=MESH)

    def dp_copy(j):
        return pltpu.make_async_remote_copy(
            src_ref=part.at[j], dst_ref=other.at[j],
            send_sem=dp_send.at[j], recv_sem=dp_recv.at[j],
            device_id={"dp": 1 - replica}, device_id_type=MESH)

    def y_copy(j):
        return pltpu.make_async_remote_copy(
            src_ref=ysend.at[j], dst_ref=yland.at[j],
            send_sem=y_send.at[j], recv_sem=y_recv.at[j],
            device_id={"mp": 2 * half + 1 - parity}, device_id_type=MESH)

    def mp_copy(j, k):
        owner = lax.rem(half + k, halves)
        return pltpu.make_async_remote_copy(
            src_ref=share.at[j, owner], dst_ref=landed.at[j, half],
            send_sem=mp_send, recv_sem=mp_recv.at[j],
            device_id={"mp": 2 * owner + parity}, device_id_type=MESH)

    def mp_all(j):
        return pltpu.make_async_remote_copy(
            src_ref=share.at[:, pl.ds(0, halves - 1)], dst_ref=landed.at[j, pl.ds(0, halves - 1)],
            send_sem=mp_send, recv_sem=mp_recv.at[j],
            device_id={"mp": lax.rem(me + 2, n_mp)}, device_id_type=MESH)

    barrier = pltpu.get_barrier_semaphore()

    @pl.loop(1, n_mp)
    def _(k):
        pl.semaphore_signal(barrier, inc=1, device_id={"mp": peer(k)}, device_id_type=MESH)

    pl.semaphore_signal(barrier, inc=1, device_id={"dp": 1 - replica}, device_id_type=MESH)

    @pl.when(sends_back)
    def _():
        @pl.loop(0, n_mp)
        def _(p):
            pl.semaphore_signal(
                barrier, inc=1, device_id={"section": section - 1, "mp": p}, device_id_type=MESH)

    @pl.when(gets_back)
    def _():
        @pl.loop(0, n_mp)
        def _(p):
            pl.semaphore_signal(
                barrier, inc=1, device_id={"section": section + 1, "mp": p}, device_id_type=MESH)

    for c in range(columns):
        both[c, :, 0] = acts_ref[c]
        both[c, :, 1] = grads_ref[c]

    neighbours = (section > 0).astype(jnp.int32) + (section < n_section - 1).astype(jnp.int32)
    pl.semaphore_wait(barrier, n_mp + n_mp * neighbours)

    @pl.loop(0, columns)
    def _(c):
        @pl.loop(1, n_mp)
        def _(k):
            col_copy(c, k).start()

    for c in range(columns):
        cols[c, me] = both[c, me]

    total[...] = jnp.zeros_like(total)

    @pl.when(jnp.logical_not(gets_back))
    def _():
        got_ref[...] = jnp.zeros_like(got_ref)

    @pl.loop(0, columns)
    def _(c):
        col_all(c).wait_recv()
        standard, inverse = normalize(cols[c, :, 0].reshape(tokens, width).astype(F32))
        normed = standard.astype(BF16)
        out_flat = cols[c, :, 1].reshape(tokens, width)
        lefts[0, c] = normed
        lefts[1, c] = out_flat
        query, key, value = (
            jnp.dot(normed, w_ref[n], preferred_element_type=F32).astype(BF16) for n in range(3))
        delta = jnp.dot(out_flat, w_ref[3], preferred_element_type=F32).astype(BF16)
        for t in range(query.shape[1] // LANES):
            cut = slice(t * LANES, (t + 1) * LANES)
            results = attend_pair(query[:, cut], key[:, cut], value[:, cut], delta[:, cut])
            for n in range(4):
                rights[n, c, :, cut] = results[n]

        if columns > 1:
            @pl.when(c < columns - 1)
            def _():
                for n in range(rights.shape[0]):
                    grad = t_dot(lefts[n // 3, c], rights[n, c])
                    total[n] += grad

        @pl.when(sends_back)
        def _():
            normed_grad = dot_t(rights[0, c], w_ref[0])
            normed_grad += dot_t(rights[1, c], w_ref[1])
            normed_grad += dot_t(rights[2, c], w_ref[2])
            branch = norm_backward(normed_grad, standard, inverse).astype(BF16)
            grad_in = (out_flat.astype(F32) + branch.astype(F32)).astype(BF16)
            back[c] = grad_in.reshape(n_mp, seqs, width)

            @pl.loop(0, n_mp)
            def _(p):
                back_copy(c, p).start()

    def weight_grad(slot, into, j):
        grad = t_dot(lefts[slot // 3, columns - 1], rights[slot, columns - 1])
        if columns > 1:
            grad = grad + total[slot]
        by_owner = grad.reshape(halves, 2, rows, grad.shape[1]).astype(into.dtype)
        for y in range(2):
            into[j, y] = by_owner[:, y]

    for j in range(slots):
        weight_grad((1 - replica) * slots + j, part, j)
        dp_copy(j).start()
    for j in range(slots):
        weight_grad(replica * slots + j, mine, j)
    for j in range(slots):
        dp_copy(j).wait()
        ysend[j] = (mine[j, 1 - parity] + other[j, 1 - parity].astype(F32)).astype(BF16)
        y_copy(j).start()
        mine[j, parity] += other[j, parity].astype(F32)
    for j in range(slots):
        y_copy(j).wait()
        summed = mine[j, parity] + yland[j].astype(F32)
        mine[j, parity] = summed
        share[j] = summed.astype(share.dtype)

        @pl.loop(1, halves)
        def _(k):
            mp_copy(j, k).start()

    for j in range(slots):
        wout_ref[j] = mine[j, parity, half]
        mp_all(j).wait_recv()

        @pl.loop(1, halves)
        def _(k):
            wout_ref[j] += landed[j, lax.rem(half + halves - k, halves)].astype(F32)

    @pl.when(gets_back)
    def _():
        back_all().wait_recv()

    @pl.when(sends_back)
    def _():
        back_all().wait_send()

    col_all(0).wait_send()
    mp_all(0).wait_send()


def per_device_kernel(activations, out_grads, layer_weights):
    n_mp, n_section, n_dp = (lax.axis_size(name) for name in ("mp", "section", "dp"))
    _, _, seqs, residues, width = activations.shape
    columns = residues // n_mp
    head_width = layer_weights.shape[3]
    tokens = n_mp * seqs
    kinds = layer_weights.shape[1]
    slots, rows = kinds // n_dp, width // n_mp

    def by_column(array):
        cut = array.reshape(seqs, n_mp, columns, width)
        return cut.transpose(2, 1, 0, 3)

    vmem = pl.BlockSpec(memory_space=pltpu.VMEM)
    dma = pltpu.SemaphoreType.DMA
    pieces = (slots, 2, n_mp // 2, rows, head_width)
    half_pieces = (slots, n_mp // 2, rows, head_width)
    got, weight_grads = pl.pallas_call(
        functools.partial(kernel, n_mp, n_section, n_dp),
        out_shape=(
            jax.ShapeDtypeStruct((columns, n_mp, seqs, width), BF16),
            jax.ShapeDtypeStruct((slots, rows, head_width), F32),
        ),
        in_specs=[vmem] * 3,
        out_specs=(vmem, vmem),
        scratch_shapes=[
            pltpu.VMEM((columns, n_mp, 2, seqs, width), BF16),
            pltpu.VMEM((columns, n_mp, 2, seqs, width), BF16),
            pltpu.VMEM((2, columns, tokens, width), BF16),
            pltpu.VMEM((kinds, columns, tokens, head_width), BF16),
            pltpu.VMEM((columns, n_mp, seqs, width), BF16),
            pltpu.VMEM(pieces, BF16),
            pltpu.VMEM(pieces, BF16),
            pltpu.VMEM(pieces, F32),
            pltpu.VMEM(half_pieces, BF16),
            pltpu.VMEM(half_pieces, BF16),
            pltpu.VMEM((kinds, width, head_width), F32),
            pltpu.VMEM(half_pieces, BF16),
            pltpu.VMEM(half_pieces, BF16),
            dma,
            dma((columns,)),
            dma,
            dma,
            dma((slots,)),
            dma((slots,)),
            dma,
            dma((slots,)),
            dma((slots,)),
            dma((slots,)),
        ],
        compiler_params=pltpu.CompilerParams(
            collective_id=0, has_side_effects=True, vmem_limit_bytes=48 * 1024 * 1024),
    )(by_column(activations), by_column(out_grads), layer_weights[0])
    received = got.transpose(2, 1, 0, 3).reshape(activations.shape)
    return received, weight_grads[None]


def per_device(activations, out_grads, layer_weights):
    n_mp, n_dp = lax.axis_size("mp"), lax.axis_size("dp")
    _, kinds, width, head_width = layer_weights.shape
    fits = (
        n_dp == 2
        and kinds % n_dp == 0
        and n_mp % 2 == 0
        and activations.shape[2] % ROWS == 0
        and (width // n_mp) % ROWS == 0
        and head_width % LANES == 0
    )
    body = per_device_kernel if fits else per_device_plain
    return body(activations, out_grads, layer_weights)


def solution(mesh):
    in_specs = (
        P("dp", "section", "mp", None, None),
        P("dp", "section", "mp", None, None),
        P("section", None, None, None),
    )
    out_specs = (P("dp", "section", "mp", None, None), P("section", "dp", "mp", None))
    return jax.shard_map(
        per_device, mesh=mesh, in_specs=in_specs, out_specs=out_specs, check_vma=False
    )
```

```python
import functools

import jax
import jax.numpy as jnp
from jax import lax
from jax.experimental import pallas as pl
from jax.experimental.pallas import tpu as pltpu
from jax.sharding import PartitionSpec as P

HEAD_DIM = 64


EPS = 1e-05


def passed_along(array, axis, by):
    peers = lax.axis_size(axis)
    pairs = [(i, i + by) for i in range(peers) if 0 <= i + by < peers]
    return lax.ppermute(array, axis, pairs)


def normalize(values):
    mean_value = jnp.mean(values, axis=-1, keepdims=True)
    centred = values - mean_value
    inverse = lax.rsqrt(jnp.mean(centred * centred, axis=-1, keepdims=True) + EPS)
    return (centred * inverse, inverse)


def norm_backward(grad_in, standard, inverse):
    grad_mean = jnp.mean(grad_in, axis=-1, keepdims=True)
    grad_proj = jnp.mean(grad_in * standard, axis=-1, keepdims=True)
    return inverse * (grad_in - grad_mean - standard * grad_proj)


def attend(queries, key_rows, values_in, out_delta):
    seq_count, res_count, head_width = queries.shape
    head_shape = (seq_count, res_count, head_width // HEAD_DIM, HEAD_DIM)
    query_heads = queries.reshape(head_shape)
    key_heads = key_rows.reshape(head_shape)
    value_heads = values_in.reshape(head_shape)
    delta_heads = out_delta.reshape(head_shape)
    scaling = HEAD_DIM ** (-0.5)
    scores = (
        jnp.einsum("srhe,trhe->rhst", query_heads, key_heads, preferred_element_type=jnp.float32)
        * scaling
    )
    row_max = jnp.max(scores, axis=-1, keepdims=True)
    exponent = jnp.exp(scores - row_max)
    probs = exponent / jnp.sum(exponent, axis=-1, keepdims=True)
    soft = probs.astype(jnp.bfloat16)
    attn_out = jnp.einsum(
        "rhst,trhe->srhe", soft, value_heads, preferred_element_type=jnp.float32
    ).astype(jnp.bfloat16)
    dprobs = jnp.einsum(
        "srhe,trhe->rhst", delta_heads, value_heads, preferred_element_type=jnp.float32
    )
    row_delta = jnp.sum(probs * dprobs, axis=-1, keepdims=True)
    dscores = (probs * (dprobs - row_delta)).astype(jnp.bfloat16)
    query_grad = (
        jnp.einsum("rhst,trhe->srhe", dscores, key_heads, preferred_element_type=jnp.float32)
        * scaling
    ).astype(jnp.bfloat16)
    key_grad = (
        jnp.einsum("rhst,srhe->trhe", dscores, query_heads, preferred_element_type=jnp.float32)
        * scaling
    ).astype(jnp.bfloat16)
    value_grad = jnp.einsum(
        "rhst,srhe->trhe", soft, delta_heads, preferred_element_type=jnp.float32
    ).astype(jnp.bfloat16)
    flat_shape = (seq_count, res_count, head_width)
    return (
        attn_out.reshape(flat_shape),
        jnp.stack(
            [
                query_grad.reshape(flat_shape),
                key_grad.reshape(flat_shape),
                value_grad.reshape(flat_shape),
            ]
        ),
    )


def input_gradient(dprojected, weight, standard, inverse, out_flat):
    normed_grad = jnp.einsum(
        "nth,ndh->td", dprojected, weight[:3], preferred_element_type=jnp.float32
    )
    branch = lax.optimization_barrier(
        norm_backward(normed_grad, standard, inverse).astype(jnp.bfloat16)
    )
    return (out_flat.astype(jnp.float32) + branch.astype(jnp.float32)).astype(jnp.bfloat16)


def per_device_plain(activations, out_grads, layer_weights):
    weight = layer_weights[0]
    model_width = activations.shape[4]
    head_width = weight.shape[2]
    col_acts, col_grads = (
        lax.all_to_all(activations, "mp", split_axis=3, concat_axis=2, tiled=True),
        lax.all_to_all(out_grads, "mp", split_axis=3, concat_axis=2, tiled=True),
    )
    seq_count, res_count = (col_acts.shape[2], col_acts.shape[3])
    tokens = seq_count * res_count
    standard, inverse = normalize(col_acts.reshape(tokens, model_width).astype(jnp.float32))
    normed = standard.astype(jnp.bfloat16)
    out_flat = col_grads.reshape(tokens, model_width)
    projected = jnp.einsum(
        "td,ndh->nth", normed, weight[:3], preferred_element_type=jnp.float32
    ).astype(jnp.bfloat16)
    attn_grad = jnp.dot(out_flat, weight[3], preferred_element_type=jnp.float32).astype(
        jnp.bfloat16
    )
    grid_shape = (seq_count, res_count, head_width)
    attn_out, stacked_grads = attend(
        projected[0].reshape(grid_shape),
        projected[1].reshape(grid_shape),
        projected[2].reshape(grid_shape),
        attn_grad.reshape(grid_shape),
    )
    dprojected = stacked_grads.reshape(3, tokens, head_width)
    attn_flat = attn_out.reshape(tokens, head_width)
    input_grad = input_gradient(dprojected, weight, standard, inverse, out_flat)
    row_grads = lax.all_to_all(
        input_grad.reshape(col_acts.shape), "mp", split_axis=2, concat_axis=3, tiled=True
    )
    received = passed_along(row_grads, "section", -1)
    projection_terms = jnp.einsum(
        "td,nth->ndh", normed, dprojected, preferred_element_type=jnp.float32
    )
    output_term = jnp.einsum("td,th->dh", out_flat, attn_flat, preferred_element_type=jnp.float32)
    grad_term = jnp.concatenate([projection_terms, output_term[None]], axis=0)[None]
    model_part = lax.psum_scatter(grad_term, "mp", scatter_dimension=2, tiled=True)
    replica_part = lax.psum_scatter(model_part, "dp", scatter_dimension=1, tiled=True)
    return (received, replica_part)


MESH = pl.DeviceIdType.MESH
LANES = 128
ROWS = 16
F32 = jnp.float32
BF16 = jnp.bfloat16


def dot_t(left, right):
    return lax.dot_general(left, right, (((1,), (1,)), ((), ())), preferred_element_type=F32)


def t_dot(left, right):
    return lax.dot_general(left, right, (((0,), (0,)), ((), ())), preferred_element_type=F32)


def attend_pair(query, key, value, delta):
    count = LANES // HEAD_DIM
    seqs = query.shape[0]
    scaling = HEAD_DIM ** (-0.5)
    lane = lax.broadcasted_iota(jnp.int32, (seqs, LANES), 1)
    masks = [(lane >= h * HEAD_DIM) & (lane < (h + 1) * HEAD_DIM) for h in range(count)]
    zero = jnp.zeros_like(key)
    keys = jnp.concatenate([jnp.where(m, key, zero) for m in masks], axis=0)
    values = jnp.concatenate([jnp.where(m, value, zero) for m in masks], axis=0)
    scores = dot_t(query, keys)
    dprobs = dot_t(delta, values)
    softs, dscores = [], []
    for h in range(count):
        cut = slice(h * seqs, (h + 1) * seqs)
        score = scores[:, cut] * scaling
        exponent = jnp.exp(score - jnp.max(score, axis=-1, keepdims=True))
        probs = exponent * (1.0 / jnp.sum(exponent, axis=-1, keepdims=True))
        dprob = dprobs[:, cut]
        row_delta = jnp.sum(probs * dprob, axis=-1, keepdims=True)
        softs.append(probs.astype(BF16))
        dscores.append((probs * (dprob - row_delta)).astype(BF16))
    soft = jnp.concatenate(softs, axis=1)
    dscore = jnp.concatenate(dscores, axis=1)
    out = jnp.dot(soft, values, preferred_element_type=F32)
    query_grad = jnp.dot(dscore, keys, preferred_element_type=F32) * scaling
    key_grad = t_dot(dscores[0], query)
    value_grad = t_dot(softs[0], delta)
    for h in range(1, count):
        key_grad = jnp.where(masks[h], t_dot(dscores[h], query), key_grad)
        value_grad = jnp.where(masks[h], t_dot(softs[h], delta), value_grad)
    key_grad = key_grad * scaling
    return query_grad.astype(BF16), key_grad.astype(BF16), value_grad.astype(BF16), out.astype(BF16)


def kernel(
    n_mp, n_section, n_dp, acts_ref, grads_ref, w_ref, got_ref, wout_ref,
    both, cols, lefts, rights, back, part, other, mine, share, landed, total, ysend, yland,
    col_send, col_recv, back_send, back_recv, dp_send, dp_recv, mp_send, mp_recv, y_send, y_recv,
):
    me = lax.axis_index("mp")
    section = lax.axis_index("section")
    replica = lax.axis_index("dp")
    columns, _, seqs, width = acts_ref.shape
    tokens = n_mp * seqs
    slots = wout_ref.shape[0]
    rows = wout_ref.shape[1]
    lane_tiles = wout_ref.shape[2] // LANES
    sends_back = section > 0
    gets_back = section < n_section - 1
    halves = n_mp // 2
    half, parity = me // 2, lax.rem(me, 2)

    def peer(k):
        return lax.rem(me + k, n_mp)

    def source(k):
        return lax.rem(me + n_mp - k, n_mp)

    others = pl.ds(0, n_mp - 1)

    def col_copy(c, k):
        return pltpu.make_async_remote_copy(
            src_ref=both.at[c, peer(k)], dst_ref=cols.at[c, me],
            send_sem=col_send, recv_sem=col_recv.at[c],
            device_id={"mp": peer(k)}, device_id_type=MESH)

    def col_all(c):
        return pltpu.make_async_remote_copy(
            src_ref=both.at[:, others], dst_ref=cols.at[c, others],
            send_sem=col_send, recv_sem=col_recv.at[c],
            device_id={"mp": peer(1)}, device_id_type=MESH)

    def back_copy(c, p):
        return pltpu.make_async_remote_copy(
            src_ref=back.at[c, p], dst_ref=got_ref.at[c, me],
            send_sem=back_send, recv_sem=back_recv,
            device_id={"section": jnp.maximum(section - 1, 0), "mp": p}, device_id_type=MESH)

    def back_all():
        return pltpu.make_async_remote_copy(
            src_ref=back, dst_ref=got_ref, send_sem=back_send, recv_sem=back_recv,
            device_id={"section": jnp.maximum(section - 1, 0)}, device_id_type=MESH)

    def dp_copy(j):
        return pltpu.make_async_remote_copy(
            src_ref=part.at[j], dst_ref=other.at[j],
            send_sem=dp_send.at[j], recv_sem=dp_recv.at[j],
            device_id={"dp": 1 - replica}, device_id_type=MESH)

    def lanes(t):
        return pl.ds(t * LANES, LANES)

    def y_copy(j, t):
        return pltpu.make_async_remote_copy(
            src_ref=ysend.at[j, :, :, lanes(t)], dst_ref=yland.at[j, :, :, lanes(t)],
            send_sem=y_send.at[j, t], recv_sem=y_recv.at[j, t],
            device_id={"mp": 2 * half + 1 - parity}, device_id_type=MESH)

    def mp_copy(j, t, k):
        owner = lax.rem(half + k, halves)
        return pltpu.make_async_remote_copy(
            src_ref=share.at[j, owner, :, lanes(t)], dst_ref=landed.at[j, half, :, lanes(t)],
            send_sem=mp_send, recv_sem=mp_recv.at[j],
            device_id={"mp": 2 * owner + parity}, device_id_type=MESH)

    def mp_all(j):
        return pltpu.make_async_remote_copy(
            src_ref=share.at[:, pl.ds(0, halves - 1)], dst_ref=landed.at[j, pl.ds(0, halves - 1)],
            send_sem=mp_send, recv_sem=mp_recv.at[j],
            device_id={"mp": lax.rem(me + 2, n_mp)}, device_id_type=MESH)

    barrier = pltpu.get_barrier_semaphore()

    @pl.loop(1, n_mp)
    def _(k):
        pl.semaphore_signal(barrier, inc=1, device_id={"mp": peer(k)}, device_id_type=MESH)

    pl.semaphore_signal(barrier, inc=1, device_id={"dp": 1 - replica}, device_id_type=MESH)

    @pl.when(sends_back)
    def _():
        @pl.loop(0, n_mp)
        def _(p):
            pl.semaphore_signal(
                barrier, inc=1, device_id={"section": section - 1, "mp": p}, device_id_type=MESH)

    @pl.when(gets_back)
    def _():
        @pl.loop(0, n_mp)
        def _(p):
            pl.semaphore_signal(
                barrier, inc=1, device_id={"section": section + 1, "mp": p}, device_id_type=MESH)

    for c in range(columns):
        both[c, :, 0] = acts_ref[c]
        both[c, :, 1] = grads_ref[c]

    neighbours = (section > 0).astype(jnp.int32) + (section < n_section - 1).astype(jnp.int32)
    pl.semaphore_wait(barrier, n_mp + n_mp * neighbours)

    @pl.loop(0, columns)
    def _(c):
        @pl.loop(1, n_mp)
        def _(k):
            col_copy(c, k).start()

    for c in range(columns):
        cols[c, me] = both[c, me]

    total[...] = jnp.zeros_like(total)

    @pl.when(jnp.logical_not(gets_back))
    def _():
        got_ref[...] = jnp.zeros_like(got_ref)

    @pl.loop(0, columns)
    def _(c):
        col_all(c).wait_recv()
        standard, inverse = normalize(cols[c, :, 0].reshape(tokens, width).astype(F32))
        normed = standard.astype(BF16)
        out_flat = cols[c, :, 1].reshape(tokens, width)
        lefts[0, c] = normed
        lefts[1, c] = out_flat
        query, key, value = (
            jnp.dot(normed, w_ref[n], preferred_element_type=F32).astype(BF16) for n in range(3))
        delta = jnp.dot(out_flat, w_ref[3], preferred_element_type=F32).astype(BF16)
        for t in range(query.shape[1] // LANES):
            cut = slice(t * LANES, (t + 1) * LANES)
            results = attend_pair(query[:, cut], key[:, cut], value[:, cut], delta[:, cut])
            for n in range(4):
                rights[n, c, :, cut] = results[n]

        if columns > 1:
            @pl.when(c < columns - 1)
            def _():
                for n in range(rights.shape[0]):
                    grad = t_dot(lefts[n // 3, c], rights[n, c])
                    total[n] += grad

        @pl.when(sends_back)
        def _():
            normed_grad = dot_t(rights[0, c], w_ref[0])
            normed_grad += dot_t(rights[1, c], w_ref[1])
            normed_grad += dot_t(rights[2, c], w_ref[2])
            branch = norm_backward(normed_grad, standard, inverse).astype(BF16)
            grad_in = (out_flat.astype(F32) + branch.astype(F32)).astype(BF16)
            back[c] = grad_in.reshape(n_mp, seqs, width)

            @pl.loop(0, n_mp)
            def _(p):
                back_copy(c, p).start()

    def weight_grad(slot, into, j):
        grad = t_dot(lefts[slot // 3, columns - 1], rights[slot, columns - 1])
        if columns > 1:
            grad = grad + total[slot]
        by_owner = grad.reshape(halves, 2, rows, grad.shape[1]).astype(into.dtype)
        for y in range(2):
            into[j, y] = by_owner[:, y]

    for j in range(slots):
        weight_grad((1 - replica) * slots + j, part, j)
        dp_copy(j).start()
    for j in range(slots):
        weight_grad(replica * slots + j, mine, j)
    for j in range(slots):
        dp_copy(j).wait()
        ysend[j] = (mine[j, 1 - parity] + other[j, 1 - parity].astype(F32)).astype(BF16)
        for t in range(lane_tiles):
            y_copy(j, t).start()
        mine[j, parity] += other[j, parity].astype(F32)
    for j in range(slots):
        for t in range(lane_tiles):
            y_copy(j, t).wait()
            summed = mine[j, parity, :, :, lanes(t)] + yland[j, :, :, lanes(t)].astype(F32)
            mine[j, parity, :, :, lanes(t)] = summed
            share[j, :, :, lanes(t)] = summed.astype(share.dtype)
            for k in range(1, halves):
                mp_copy(j, t, k).start()

    for j in range(slots):
        wout_ref[j] = mine[j, parity, half]
        mp_all(j).wait_recv()

        @pl.loop(1, halves)
        def _(k):
            wout_ref[j] += landed[j, lax.rem(half + halves - k, halves)].astype(F32)

    @pl.when(gets_back)
    def _():
        back_all().wait_recv()

    @pl.when(sends_back)
    def _():
        back_all().wait_send()

    col_all(0).wait_send()
    mp_all(0).wait_send()


def per_device_kernel(activations, out_grads, layer_weights):
    n_mp, n_section, n_dp = (lax.axis_size(name) for name in ("mp", "section", "dp"))
    _, _, seqs, residues, width = activations.shape
    columns = residues // n_mp
    head_width = layer_weights.shape[3]
    tokens = n_mp * seqs
    kinds = layer_weights.shape[1]
    slots, rows = kinds // n_dp, width // n_mp

    def by_column(array):
        cut = array.reshape(seqs, n_mp, columns, width)
        return cut.transpose(2, 1, 0, 3)

    vmem = pl.BlockSpec(memory_space=pltpu.VMEM)
    dma = pltpu.SemaphoreType.DMA
    pieces = (slots, 2, n_mp // 2, rows, head_width)
    half_pieces = (slots, n_mp // 2, rows, head_width)
    got, weight_grads = pl.pallas_call(
        functools.partial(kernel, n_mp, n_section, n_dp),
        out_shape=(
            jax.ShapeDtypeStruct((columns, n_mp, seqs, width), BF16),
            jax.ShapeDtypeStruct((slots, rows, head_width), F32),
        ),
        in_specs=[vmem] * 3,
        out_specs=(vmem, vmem),
        scratch_shapes=[
            pltpu.VMEM((columns, n_mp, 2, seqs, width), BF16),
            pltpu.VMEM((columns, n_mp, 2, seqs, width), BF16),
            pltpu.VMEM((2, columns, tokens, width), BF16),
            pltpu.VMEM((kinds, columns, tokens, head_width), BF16),
            pltpu.VMEM((columns, n_mp, seqs, width), BF16),
            pltpu.VMEM(pieces, BF16),
            pltpu.VMEM(pieces, BF16),
            pltpu.VMEM(pieces, F32),
            pltpu.VMEM(half_pieces, BF16),
            pltpu.VMEM(half_pieces, BF16),
            pltpu.VMEM((kinds, width, head_width), F32),
            pltpu.VMEM(half_pieces, BF16),
            pltpu.VMEM(half_pieces, BF16),
            dma,
            dma((columns,)),
            dma,
            dma,
            dma((slots,)),
            dma((slots,)),
            dma,
            dma((slots,)),
            dma((slots, head_width // LANES)),
            dma((slots, head_width // LANES)),
        ],
        compiler_params=pltpu.CompilerParams(
            collective_id=0, has_side_effects=True, vmem_limit_bytes=48 * 1024 * 1024),
    )(by_column(activations), by_column(out_grads), layer_weights[0])
    received = got.transpose(2, 1, 0, 3).reshape(activations.shape)
    return received, weight_grads[None]


def per_device(activations, out_grads, layer_weights):
    n_mp, n_dp = lax.axis_size("mp"), lax.axis_size("dp")
    _, kinds, width, head_width = layer_weights.shape
    fits = (
        n_dp == 2
        and kinds % n_dp == 0
        and n_mp % 2 == 0
        and activations.shape[2] % ROWS == 0
        and (width // n_mp) % ROWS == 0
        and head_width % LANES == 0
    )
    body = per_device_kernel if fits else per_device_plain
    return body(activations, out_grads, layer_weights)


def solution(mesh):
    in_specs = (
        P("dp", "section", "mp", None, None),
        P("dp", "section", "mp", None, None),
        P("section", None, None, None),
    )
    out_specs = (P("dp", "section", "mp", None, None), P("section", "dp", "mp", None))
    return jax.shard_map(
        per_device, mesh=mesh, in_specs=in_specs, out_specs=out_specs, check_vma=False
    )
```
